32 devices in a mesh: row: 4 (over y, core), col: 8 (over z, x).
Axes of the slice: x: 2, y: 2, z: 4, core: 2. Of those that a mesh axis runs over, the one named last changes fastest.
Arguments:
- tokens: bfloat16 [1024, 8192], P('col', 'row'), may hold values from -6 to 6
- query_weight: bfloat16 [8192, 8192], P('row', 'col'), may hold values from -0.0625 to 0.0625
- key_weight: bfloat16 [8192, 8192], P('row', 'col'), may hold values from -0.0625 to 0.0625
- value_weight: bfloat16 [8192, 8192], P('row', 'col'), may hold values from -0.0625 to 0.0625
- out_weight: bfloat16 [8192, 8192], P('col', 'row'), may hold values from -0.0625 to 0.0625
- filter_taps: float32 [7, 512], P(None, 'col'), may hold values from -4 to 4
- out_grad: bfloat16 [1024, 8192], P('col', 'row'), may hold values from -6 to 6
Outputs:
- block_out: bfloat16 [1024, 8192], P('col', 'row')
- tokens_grad: bfloat16 [1024, 8192], P('col', 'row')
- query_grad: bfloat16 [8192, 8192], P('row', 'col')
- key_grad: bfloat16 [8192, 8192], P('row', 'col')
- value_grad: bfloat16 [8192, 8192], P('row', 'col')
- outw_grad: bfloat16 [8192, 8192], P('col', 'row')
- taps_grad: float32 [7, 512], P(None, 'col')
The draws below stay inside these ranges and needn't reach their ends.
All inputs are finite; a program needn't handle non-finite values.
Results may differ from the reference program's by a relative error of at most 0.035.
Values may be sent and summed in bfloat16 or wider, within the bound.
A program may use at most 128 MiB of HBM per device.

```python
import jax
import jax.numpy as jnp
from jax import lax

D = 8192
KW = 7
GROUP = 16
TOKENS = 1024
LENGTH = 1024
GROUPS = 512
N_ROW = 4


def shard_levels(key, extent, split, least, top_value):
    loudness, own = 1.0, jax.random.fold_in(key, 6)
    for axis_at, shards_of in split:
        draws = jnp.exp(jax.random.uniform(jax.random.fold_in(own, axis_at), (shards_of,), jnp.float32, least / len(split), top_value / len(split)))
        loudness = loudness * jnp.repeat(draws, extent[axis_at] // shards_of).reshape([-1 if axis == axis_at else 1 for axis in range(len(extent))])
    return loudness


def centred(own_key, shape, scale, most, split=(), kind=jnp.bfloat16):
    result = scale * jax.random.normal(own_key, shape, jnp.float32)
    if split:
        result = result * shard_levels(own_key, shape, split, -0.22, 0.18)
    return jnp.clip(result, -most, most).astype(kind)


def setup_inputs(seed: int = 0) -> dict:
    splits = jax.random.split(jax.random.key(seed), 8)
    return {
        "tokens": centred(splits[0], (TOKENS, D), 1.0, 6.0, ((0, 8), (1, 4))),
        "query_weight": centred(splits[1], (D, D), D ** -0.5, 0.0625, ((0, 4), (1, 8))),
        "key_weight": centred(splits[2], (D, D), D ** -0.5, 0.0625, ((0, 4), (1, 8))),
        "value_weight": centred(splits[3], (D, D), D ** -0.5, 0.0625, ((0, 4), (1, 8))),
        "out_weight": centred(splits[4], (D, D), D ** -0.5, 0.0625, ((0, 8), (1, 4))),
        "filter_taps": centred(splits[5], (KW, GROUPS), 0.4, 4.0, ((1, 8),), jnp.float32),
        "out_grad": centred(splits[6], (TOKENS, D), 1.0, 6.0, ((0, 8), (1, 4))),
    }


def causal_conv(signal, taps, positions):
    count_rows = signal.shape[0]
    padded = jnp.pad(signal, ((KW - 1, 0), (0, 0)))
    total = jnp.zeros(signal.shape, jnp.float32)
    for offset in range(KW):
        shifted = padded[KW - 1 - offset:KW - 1 - offset + count_rows]
        keep = (positions % LENGTH >= offset)[:, None]
        total = total + jnp.where(keep, taps[offset][None, :] * shifted, 0.0)
    return total


def causal_conv_back(cotangent, taps, positions):
    count_rows = cotangent.shape[0]
    padded = jnp.pad(cotangent, ((0, KW - 1), (0, 0)))
    total = jnp.zeros(cotangent.shape, jnp.float32)
    for offset in range(KW):
        shifted = padded[offset:offset + count_rows]
        keep = ((positions % LENGTH) + offset < LENGTH)[:, None]
        total = total + jnp.where(keep, taps[offset][None, :] * shifted, 0.0)
    return total


def blockwise(left, right_fn, width_out):
    block = D // N_ROW
    total = jnp.zeros((left.shape[0], width_out), jnp.float32)
    for shard in range(N_ROW):
        partial_value = right_fn(left[:, shard * block:(shard + 1) * block], shard * block, block).astype(jnp.bfloat16)
        total = total + lax.optimization_barrier(partial_value).astype(jnp.float32)
    return total.astype(jnp.bfloat16)


def reference(tokens, query_weight, key_weight, value_weight, out_weight, filter_taps, out_grad):
    def projector(weight):
        def apply(columns, first, width):
            return jnp.dot(columns, weight[first:first + width], preferred_element_type=jnp.float32)
        return apply

    query = blockwise(tokens, projector(query_weight), D)
    keys = blockwise(tokens, projector(key_weight), D)
    values = blockwise(tokens, projector(value_weight), D)
    product = (keys.astype(jnp.float32) * values.astype(jnp.float32)).astype(jnp.bfloat16)
    taps = jnp.repeat(filter_taps.astype(jnp.float32), GROUP, axis=1)
    positions = jnp.arange(TOKENS, dtype=jnp.int32)
    conv_out = causal_conv(product.astype(jnp.float32), taps, positions).astype(jnp.bfloat16)
    gated = (query.astype(jnp.float32) * conv_out.astype(jnp.float32)).astype(jnp.bfloat16)
    block_out = jnp.dot(gated, out_weight, preferred_element_type=jnp.float32).astype(jnp.bfloat16)

    def back_apply(columns, first, width):
        return jnp.dot(columns, out_weight[:, first:first + width].T, preferred_element_type=jnp.float32)

    gated_grad = blockwise(out_grad, back_apply, D)
    query_back = (gated_grad.astype(jnp.float32) * conv_out.astype(jnp.float32)).astype(jnp.bfloat16)
    conv_grad = (gated_grad.astype(jnp.float32) * query.astype(jnp.float32)).astype(jnp.bfloat16)
    product_grad = causal_conv_back(conv_grad.astype(jnp.float32), taps, positions)
    keys_back = (product_grad * values.astype(jnp.float32)).astype(jnp.bfloat16)
    values_back = (product_grad * keys.astype(jnp.float32)).astype(jnp.bfloat16)

    padded = jnp.pad(product.astype(jnp.float32), ((KW - 1, 0), (0, 0)))
    rows_grad = []
    for offset in range(KW):
        shifted = padded[KW - 1 - offset:KW - 1 - offset + TOKENS]
        keep = (positions % LENGTH >= offset)[:, None]
        rows_grad.append(jnp.sum(jnp.where(keep, conv_grad.astype(jnp.float32) * shifted, 0.0), axis=0))
    taps_grad = jnp.stack(rows_grad).reshape(KW, GROUPS, GROUP).sum(axis=2)

    query_grad = jnp.dot(tokens.T, query_back, preferred_element_type=jnp.float32).astype(jnp.bfloat16)
    key_grad = jnp.dot(tokens.T, keys_back, preferred_element_type=jnp.float32).astype(jnp.bfloat16)
    value_grad = jnp.dot(tokens.T, values_back, preferred_element_type=jnp.float32).astype(jnp.bfloat16)
    outw_grad = jnp.dot(gated.T, out_grad, preferred_element_type=jnp.float32).astype(jnp.bfloat16)
    tokens_grad = (jnp.dot(query_back, query_weight.T, preferred_element_type=jnp.float32)
                   + jnp.dot(keys_back, key_weight.T, preferred_element_type=jnp.float32)
                   + jnp.dot(values_back, value_weight.T, preferred_element_type=jnp.float32)).astype(jnp.bfloat16)
    return block_out, tokens_grad, query_grad, key_grad, value_grad, outw_grad, taps_grad
```

```python
import functools

import jax
import jax.numpy as jnp
from jax import lax
from jax.experimental import pallas as pl
from jax.experimental.pallas import tpu as pltpu
from jax.sharding import PartitionSpec as P

SEQS = 1
KW = 7
GROUP = 16
Z_LINE = 4
CORES = 2
WIDE = 512
MESH = pl.DeviceIdType.MESH
VMEM_BYTES = 62 * 1024 * 1024


def contract_rows(left, right):
    return lax.dot_general(
        left, right, (((0,), (0,)), ((), ())), preferred_element_type=jnp.float32
    )


def contract_cols(left, right):
    return lax.dot_general(
        left, right, (((1,), (1,)), ((), ())), preferred_element_type=jnp.float32
    )


def push(src, dst, send, recv, axis, index):
    return pltpu.make_async_remote_copy(
        src_ref=src,
        dst_ref=dst,
        send_sem=send,
        recv_sem=recv,
        device_id={axis: index},
        device_id_type=MESH,
    )


def greet(n_col, n_row):
    col, row = lax.axis_index("col"), lax.axis_index("row")
    barrier = pltpu.get_barrier_semaphore()
    for i in range(1, n_col):
        pl.semaphore_signal(
            barrier, inc=1, device_id={"col": lax.rem(col + i, n_col)}, device_id_type=MESH
        )
    for i in range(1, n_row):
        pl.semaphore_signal(
            barrier, inc=1, device_id={"row": lax.rem(row + i, n_row)}, device_id_type=MESH
        )
    pl.semaphore_wait(barrier, n_col + n_row - 2)


def forward_kernel(
    n_col, n_row, n_z,
    tokens, grads, wq, wk, wv, wo,
    sums, tokens_all, grads_all,
    held, w_in, w_out, parts, got,
    z_send, z_recv, x_send, x_recv, r_send, r_recv, w_sem, own_sem, out_sem,
):
    n_x = n_col // n_z
    col, me = lax.axis_index("col"), lax.axis_index("row")
    z, x = col // n_x, lax.rem(col, n_x)
    hidden = w_in.shape[2]
    slice_cols = hidden // n_row
    own_copies = [
        pltpu.make_async_copy(ref, held.at[a, col], own_sem.at[a])
        for a, ref in enumerate((tokens, grads))
    ]
    for copy in own_copies:
        copy.start()
    weight_copies = [
        pltpu.make_async_copy(ref, w_in.at[m], w_sem.at[m]) for m, ref in enumerate((wq, wk, wv))
    ] + [pltpu.make_async_copy(wo, w_out, w_sem.at[3])]
    for copy in weight_copies:
        copy.start()
    greet(n_col, n_row)
    own_copies[0].wait()
    own_copies[1].wait()

    def z_copy(a, block, way):
        slot = held.at[a, block * n_x + x]
        return push(slot, slot, z_send.at[a, way, block], z_recv.at[a, block], "col",
                    (z + 1 - 2 * way) * n_x + x)

    def x_copy(a, block, source, i):
        slot = held.at[a, block * n_x + source]
        return push(slot, slot, x_send.at[a, block, i], x_recv.at[a, block, source], "col",
                    z * n_x + lax.rem(x + i, n_x))

    def out_copy(a, block):
        dst = (tokens_all, grads_all)[a]
        return pltpu.make_async_copy(held.at[a, block], dst.at[block], out_sem.at[a, block])

    def r_copy(a, block, to, source):
        which = pl.ds(0, 3) if a == 0 else pl.ds(3, 1)
        return push(parts.at[to, block, which], got.at[source, block, which],
                    r_send.at[a, to, block], r_recv.at[a, source, block], "row", to)

    def work(a, block):
        out_copy(a, block).start()

        def one(m, carry):
            rows = held[a, block]
            if a == 0:
                part = jnp.dot(rows, w_in[m], preferred_element_type=jnp.float32)
            else:
                part = contract_cols(rows, w_out[...])
            part = part.astype(jnp.bfloat16)
            for to in range(n_row):
                parts[to, block, m if a == 0 else 3] = part[:, to * slice_cols:(to + 1) * slice_cols]
            return carry

        if a == 0:
            lax.fori_loop(0, 3, one, 0)
        else:
            one(3, 0)
        for i in range(1, n_row):
            r_copy(a, block, lax.rem(me + i, n_row), me).start()

    def arrived(a, block):
        for i in range(1, n_x):
            x_copy(a, block, x, i).start()
        work(a, block * n_x + x)

        def other(i, carry):
            source = lax.rem(x + i, n_x)
            x_copy(a, block, source, 1).wait_recv()
            work(a, block * n_x + source)
            return carry

        lax.fori_loop(1, n_x, other, 0)

    for a in range(2):
        @pl.when(z + 1 < n_z)
        def _():
            z_copy(a, z, 0).start()

        @pl.when(z > 0)
        def _():
            z_copy(a, z, 1).start()

        if a == 0:
            for copy in weight_copies[:3]:
                copy.wait()
        else:
            weight_copies[3].wait()
        arrived(a, z)

        def step(s, carry):
            before, after = z - s, z + s

            @pl.when(before >= 0)
            def _():
                z_copy(a, before, 0).wait_recv()

                @pl.when(z + 1 < n_z)
                def _():
                    z_copy(a, before, 0).start()

            @pl.when(after < n_z)
            def _():
                z_copy(a, after, 1).wait_recv()

                @pl.when(z > 0)
                def _():
                    z_copy(a, after, 1).start()

            @pl.when(before >= 0)
            def _():
                arrived(a, before)

            @pl.when(after < n_z)
            def _():
                arrived(a, after)

            return carry

        lax.fori_loop(1, n_z, step, 0)

    def total(block, carry):
        for a, which in ((0, range(3)), (1, range(3, 4))):
            for i in range(1, n_row):
                r_copy(a, block, me, lax.rem(me + i, n_row)).wait_recv()
            for m in which:
                value = parts[me, block, m].astype(jnp.float32)
                for i in range(1, n_row):
                    value = value + got[lax.rem(me + i, n_row), block, m].astype(jnp.float32)
                sums[m, block] = value.astype(jnp.bfloat16)
        return carry

    lax.fori_loop(0, n_col, total, 0)

    for a in range(2):
        def finish_z(block, carry):
            @pl.when((block <= z) & (z + 1 < n_z))
            def _():
                z_copy(a, block, 0).wait_send()

            @pl.when((block >= z) & (z > 0))
            def _():
                z_copy(a, block, 1).wait_send()

            for i in range(1, n_x):
                x_copy(a, block, x, i).wait_send()
            return carry

        lax.fori_loop(0, n_z, finish_z, 0)

        def finish_block(block, carry):
            out_copy(a, block).wait()
            for i in range(1, n_row):
                r_copy(a, block, lax.rem(me + i, n_row), me).wait_send()
            return carry

        lax.fori_loop(0, n_col, finish_block, 0)


def backward_kernel(
    n_col, n_row, n_z,
    acts, wo, wq, wk, wv,
    block_out, tokens_grad, acts_all,
    held, w_out, w_in, parts, x_got, z_got,
    w_sem, own_sem, g_send, g_recv, x_send, x_recv, z_send, z_recv, out_sem,
):
    n_x, n_y = n_col // n_z, n_row // CORES
    col, me = lax.axis_index("col"), lax.axis_index("row")
    z, x = col // n_x, lax.rem(col, n_x)
    y, core = me // CORES, lax.rem(me, CORES)
    partner = y * CORES + 1 - core
    block_rows = parts.shape[2]
    features = parts.shape[3]
    own_copies = [
        pltpu.make_async_copy(acts.at[m], held.at[m, me], own_sem.at[m]) for m in range(4)
    ]
    for copy in own_copies:
        copy.start()
    weight_copies = [pltpu.make_async_copy(wo, w_out, w_sem.at[0])] + [
        pltpu.make_async_copy(ref, w_in.at[m], w_sem.at[m + 1]) for m, ref in enumerate((wq, wk, wv))
    ]
    for copy in weight_copies:
        copy.start()
    greet(n_col, n_row)

    def g_copy(m, source, slot, to):
        return push(held.at[m, source], held.at[m, source], g_send.at[m, slot],
                    g_recv.at[m, source], "row", to)

    def out_copy(m, source):
        return pltpu.make_async_copy(held.at[m, source], acts_all.at[m, source], out_sem.at[m, source])

    for m in range(4):
        own_copies[m].wait()
        for i in range(1, n_y):
            g_copy(m, me, i, lax.rem(y + i, n_y) * CORES + core).start()
        g_copy(m, me, 0, partner).start()

    def pass_on(m):
        out_copy(m, me).start()
        for i in range(1, n_y):
            source = lax.rem(y + i, n_y) * CORES + core
            g_copy(m, source, 0, partner).wait_recv()
            g_copy(m, source, n_y - 1 + i, partner).start()
            out_copy(m, source).start()

    def settle(m):
        for i in range(n_y):
            source = lax.rem(y + i, n_y) * CORES + 1 - core
            g_copy(m, source, 0, partner).wait_recv()
            out_copy(m, source).start()

    def act(m, block):
        rows = pl.ds(pl.multiple_of(block * block_rows, block_rows), block_rows)
        return jnp.concatenate([held[m, r, rows] for r in range(n_row)], axis=1)

    def x_copy(phase, block, to, source):
        return push(parts.at[phase, block * n_x + to], x_got.at[phase, source, block],
                    x_send.at[phase, block, to], x_recv.at[phase, source, block], "col",
                    z * n_x + to)

    def z_copy(phase, block, way):
        return push(parts.at[phase, block * n_x + x], z_got.at[phase, way, block],
                    z_send.at[phase, block], z_recv.at[phase, way, block], "col",
                    (z + 1 - 2 * way) * n_x + x)

    def multiply(phase, block):
        wide = min(WIDE, features)

        def tile(n, carry):
            cols = pl.ds(pl.multiple_of(n * wide, wide), wide)
            if phase == 0:
                value = jnp.dot(act(0, block), w_out[:, cols], preferred_element_type=jnp.float32)
            else:
                value = contract_cols(act(1, block), w_in[0, cols])
                value = value + contract_cols(act(2, block), w_in[1, cols])
                value = value + contract_cols(act(3, block), w_in[2, cols])
            parts[phase, block, :, cols] = value.astype(jnp.bfloat16)
            return carry

        lax.fori_loop(0, features // wide, tile, 0)

    order = []
    for k in range(n_z // 2):
        order += [n_z - 1 - k, k]

    def start_phase(phase):
        for block in order:
            def send(i, carry):
                to = lax.rem(x + i, n_x)
                multiply(phase, block * n_x + to)
                x_copy(phase, block, to, x).start()
                return carry

            lax.fori_loop(1, n_x, send, 0)
            multiply(phase, block * n_x + x)

    def x_total(phase, block):
        value = parts[phase, block * n_x + x].astype(jnp.float32)
        for i in range(1, n_x):
            source = lax.rem(x + i, n_x)
            x_copy(phase, block, x, source).wait_recv()
            value = value + x_got[phase, source, block].astype(jnp.float32)
        parts[phase, block * n_x + x] = value.astype(jnp.bfloat16)

    def add_z(phase, block, way):
        z_copy(phase, block, way).wait_recv()
        slot = block * n_x + x
        parts[phase, slot] = (
            parts[phase, slot].astype(jnp.float32) + z_got[phase, way, block].astype(jnp.float32)
        ).astype(jnp.bfloat16)

    def reduce_step(phase, block):
        x_total(phase, block)

        @pl.when(z < block)
        def _():
            @pl.when(z > 0)
            def _():
                add_z(phase, block, 0)

            z_copy(phase, block, 0).start()

        @pl.when(z > block)
        def _():
            @pl.when(z + 1 < n_z)
            def _():
                add_z(phase, block, 1)

            z_copy(phase, block, 1).start()

    def final(phase, out):
        @pl.when(z > 0)
        def _():
            add_z(phase, z, 0)

        @pl.when(z + 1 < n_z)
        def _():
            add_z(phase, z, 1)

        out[...] = parts[phase, z * n_x + x]

    pass_on(0)
    weight_copies[0].wait()
    settle(0)
    start_phase(0)
    for k, block in enumerate(order):
        if k < 3:
            pass_on(k + 1)
        reduce_step(0, block)
    for m in range(1, 4):
        settle(m)
        weight_copies[m].wait()
    start_phase(1)
    final(0, block_out)
    for block in order:
        reduce_step(1, block)
    final(1, tokens_grad)

    for m in range(4):
        for i in range(1, n_y):
            g_copy(m, me, i, partner).wait_send()
            g_copy(m, me, n_y - 1 + i, partner).wait_send()
        g_copy(m, me, 0, partner).wait_send()
        for source in range(n_row):
            out_copy(m, source).wait()
    for phase in range(2):
        def finish(block, carry):
            for i in range(1, n_x):
                x_copy(phase, block, lax.rem(x + i, n_x), x).wait_send()

            @pl.when(z != block)
            def _():
                z_copy(phase, block, 0).wait_send()

            return carry

        lax.fori_loop(0, n_z, finish, 0)


def shift_down(value, by):
    return jnp.pad(value, ((by, 0), (0, 0)))[: value.shape[0]] if by else value


def shift_up(value, by):
    return jnp.pad(value, ((0, by), (0, 0)))[by:] if by else value


def local(tokens, query_weight, key_weight, value_weight, out_weight, filter_taps, out_grad):
    n_row, n_col = lax.axis_size("row"), lax.axis_size("col")
    me = lax.axis_index("row")
    n_z, n_x, n_y = Z_LINE, n_col // Z_LINE, n_row // CORES
    block_rows, features = tokens.shape
    hidden = query_weight.shape[1]
    total_tokens = block_rows * n_col
    slice_cols = hidden // n_row
    bf16 = jnp.bfloat16
    anywhere = pl.BlockSpec(memory_space=pl.ANY)
    inside = pl.BlockSpec(memory_space=pltpu.VMEM)
    dma = pltpu.SemaphoreType.DMA
    gathered = jax.ShapeDtypeStruct((n_col, block_rows, features), bf16)
    sums, full_tokens, full_grads = pl.pallas_call(
        functools.partial(forward_kernel, n_col, n_row, n_z),
        out_shape=(
            jax.ShapeDtypeStruct((4, n_col, block_rows, slice_cols), bf16), gathered, gathered,
        ),
        in_specs=[anywhere] * 6,
        out_specs=(inside, anywhere, anywhere),
        scratch_shapes=[
            pltpu.VMEM((2, n_col, block_rows, features), bf16),
            pltpu.VMEM((3, features, hidden), bf16),
            pltpu.VMEM((hidden, features), bf16),
            pltpu.VMEM((n_row, n_col, 4, block_rows, slice_cols), bf16),
            pltpu.VMEM((n_row, n_col, 4, block_rows, slice_cols), bf16),
            dma((2, 2, n_z)), dma((2, n_z)),
            dma((2, n_z, n_x)), dma((2, n_z, n_x)),
            dma((2, n_row, n_col)), dma((2, n_row, n_col)),
            dma((4,)), dma((2,)), dma((2, n_col)),
        ],
        compiler_params=pltpu.CompilerParams(
            collective_id=0, has_side_effects=True, vmem_limit_bytes=VMEM_BYTES
        ),
        name="gather_project",
    )(tokens, out_grad, query_weight, key_weight, value_weight, out_weight)
    full_tokens = full_tokens.reshape(total_tokens, features)
    full_grads = full_grads.reshape(total_tokens, features)
    query, keys, values, gated_grad = [
        sums[m].reshape(total_tokens, slice_cols).astype(jnp.float32) for m in range(4)
    ]
    own_groups = slice_cols // GROUP
    taps = lax.dynamic_slice_in_dim(filter_taps, me * own_groups, own_groups, axis=1)
    taps = jnp.repeat(taps, GROUP, axis=1)
    product = (keys * values).astype(bf16).astype(jnp.float32)
    conv_out = sum(taps[j][None, :] * shift_down(product, j) for j in range(KW))
    conv_out = conv_out.astype(bf16).astype(jnp.float32)
    gated = (query * conv_out).astype(bf16)
    query_back = (gated_grad * conv_out).astype(bf16)
    conv_grad = (gated_grad * query).astype(bf16).astype(jnp.float32)
    product_grad = sum(taps[j][None, :] * shift_up(conv_grad, j) for j in range(KW))
    keys_back = (product_grad * values).astype(bf16)
    values_back = (product_grad * keys).astype(bf16)
    taps_rows = jnp.stack(
        [jnp.sum(conv_grad * shift_down(product, j), axis=0) for j in range(KW)]
    )
    taps_own = taps_rows.reshape(KW, own_groups, GROUP).sum(axis=2)
    taps_grad = lax.all_gather(taps_own, "row", axis=1, tiled=True)
    acts = jnp.stack([gated, query_back, keys_back, values_back])
    shard = jax.ShapeDtypeStruct((block_rows, features), bf16)
    block_out, tokens_grad, acts_all = pl.pallas_call(
        functools.partial(backward_kernel, n_col, n_row, n_z),
        out_shape=(
            shard, shard, jax.ShapeDtypeStruct((4, n_row, total_tokens, slice_cols), bf16),
        ),
        in_specs=[anywhere] * 5,
        out_specs=(inside, inside, anywhere),
        scratch_shapes=[
            pltpu.VMEM((4, n_row, total_tokens, slice_cols), bf16),
            pltpu.VMEM((hidden, features), bf16),
            pltpu.VMEM((3, features, hidden), bf16),
            pltpu.VMEM((2, n_col, block_rows, features), bf16),
            pltpu.VMEM((2, n_x, n_z, block_rows, features), bf16),
            pltpu.VMEM((2, 2, n_z, block_rows, features), bf16),
            dma((4,)), dma((4,)),
            dma((4, 2 * n_y)), dma((4, n_row)),
            dma((2, n_z, n_x)), dma((2, n_x, n_z)),
            dma((2, n_z)), dma((2, 2, n_z)),
            dma((4, n_row)),
        ],
        compiler_params=pltpu.CompilerParams(
            collective_id=1, has_side_effects=True, vmem_limit_bytes=VMEM_BYTES
        ),
        name="gather_scatter",
    )(acts, out_weight, query_weight, key_weight, value_weight)
    joined = jnp.transpose(acts_all, (0, 2, 1, 3)).reshape(4, total_tokens, hidden)
    query_grad = contract_rows(full_tokens, joined[1]).astype(bf16)
    key_grad = contract_rows(full_tokens, joined[2]).astype(bf16)
    value_grad = contract_rows(full_tokens, joined[3]).astype(bf16)
    outw_grad = contract_rows(joined[0], full_grads).astype(bf16)
    return (block_out, tokens_grad, query_grad, key_grad, value_grad, outw_grad, taps_grad)


def solution(mesh):
    in_specs = (
        P("col", "row"),
        P("row", "col"),
        P("row", "col"),
        P("row", "col"),
        P("col", "row"),
        P(None, "col"),
        P("col", "row"),
    )
    out_specs = (
        P("col", "row"),
        P("col", "row"),
        P("row", "col"),
        P("row", "col"),
        P("row", "col"),
        P("col", "row"),
        P(None, "col"),
    )
    return jax.shard_map(local, mesh=mesh, in_specs=in_specs, out_specs=out_specs, check_vma=False)
```

```python
import functools

import jax
import jax.numpy as jnp
from jax import lax
from jax.experimental import pallas as pl
from jax.experimental.pallas import tpu as pltpu
from jax.sharding import PartitionSpec as P

SEQS = 1
KW = 7
GROUP = 16
Z_LINE = 4
CORES = 2
WIDE = 512
MESH = pl.DeviceIdType.MESH
VMEM_BYTES = 62 * 1024 * 1024


def contract_rows(left, right):
    return lax.dot_general(
        left, right, (((0,), (0,)), ((), ())), preferred_element_type=jnp.float32
    )


def contract_cols(left, right):
    return lax.dot_general(
        left, right, (((1,), (1,)), ((), ())), preferred_element_type=jnp.float32
    )


def push(src, dst, send, recv, axis, index):
    return pltpu.make_async_remote_copy(
        src_ref=src,
        dst_ref=dst,
        send_sem=send,
        recv_sem=recv,
        device_id={axis: index},
        device_id_type=MESH,
    )


def greet(n_col, n_row):
    col, row = lax.axis_index("col"), lax.axis_index("row")
    barrier = pltpu.get_barrier_semaphore()
    for i in range(1, n_col):
        pl.semaphore_signal(
            barrier, inc=1, device_id={"col": lax.rem(col + i, n_col)}, device_id_type=MESH
        )
    for i in range(1, n_row):
        pl.semaphore_signal(
            barrier, inc=1, device_id={"row": lax.rem(row + i, n_row)}, device_id_type=MESH
        )
    pl.semaphore_wait(barrier, n_col + n_row - 2)


def forward_kernel(
    n_col, n_row, n_z,
    tokens, grads, wq, wk, wv, wo,
    sums, tokens_all, grads_all,
    held, w_in, w_out, parts, got,
    z_send, z_recv, x_send, x_recv, r_send, r_recv, w_sem, own_sem, out_sem,
):
    n_x = n_col // n_z
    col, me = lax.axis_index("col"), lax.axis_index("row")
    z, x = col // n_x, lax.rem(col, n_x)
    hidden = w_in.shape[2]
    slice_cols = hidden // n_row
    own_copies = [
        pltpu.make_async_copy(ref, held.at[a, col], own_sem.at[a])
        for a, ref in enumerate((tokens, grads))
    ]
    for copy in own_copies:
        copy.start()
    weight_copies = [
        pltpu.make_async_copy(ref, w_in.at[m], w_sem.at[m]) for m, ref in enumerate((wq, wk, wv))
    ] + [pltpu.make_async_copy(wo, w_out, w_sem.at[3])]
    for copy in weight_copies:
        copy.start()
    greet(n_col, n_row)
    own_copies[0].wait()
    own_copies[1].wait()

    def z_copy(a, block, way):
        slot = held.at[a, block * n_x + x]
        return push(slot, slot, z_send.at[a, way, block], z_recv.at[a, block], "col",
                    (z + 1 - 2 * way) * n_x + x)

    def x_copy(a, block, source, i):
        slot = held.at[a, block * n_x + source]
        return push(slot, slot, x_send.at[a, block, i], x_recv.at[a, block, source], "col",
                    z * n_x + lax.rem(x + i, n_x))

    def out_copy(a, block):
        dst = (tokens_all, grads_all)[a]
        return pltpu.make_async_copy(held.at[a, block], dst.at[block], out_sem.at[a, block])

    def r_copy(a, block, to, source):
        which = pl.ds(0, 3) if a == 0 else pl.ds(3, 1)
        return push(parts.at[to, block, which], got.at[source, block, which],
                    r_send.at[a, to, block], r_recv.at[a, source, block], "row", to)

    def work(a, block):
        out_copy(a, block).start()

        def one(m, carry):
            rows = held[a, block]
            if a == 0:
                part = jnp.dot(rows, w_in[m], preferred_element_type=jnp.float32)
            else:
                part = contract_cols(rows, w_out[...])
            part = part.astype(jnp.bfloat16)
            for to in range(n_row):
                parts[to, block, m if a == 0 else 3] = part[:, to * slice_cols:(to + 1) * slice_cols]
            return carry

        if a == 0:
            lax.fori_loop(0, 3, one, 0)
        else:
            one(3, 0)
        for i in range(1, n_row):
            r_copy(a, block, lax.rem(me + i, n_row), me).start()

    def spread(a, block):
        for i in range(1, n_x):
            x_copy(a, block, x, i).start()

    def others(a, block):
        def other(i, carry):
            source = lax.rem(x + i, n_x)
            x_copy(a, block, source, 1).wait_recv()
            work(a, block * n_x + source)
            return carry

        lax.fori_loop(1, n_x, other, 0)

    def begin(a):
        @pl.when(z + 1 < n_z)
        def _():
            z_copy(a, z, 0).start()

        @pl.when(z > 0)
        def _():
            z_copy(a, z, 1).start()

        spread(a, z)

    def both(s, fn):
        @pl.when(z - s >= 0)
        def _():
            fn(z - s, 0, z + 1 < n_z)

        if s != 0:
            @pl.when(z + s < n_z)
            def _():
                fn(z + s, 1, z > 0)

    begin(0)
    for a in range(2):
        for copy in weight_copies[:3] if a == 0 else weight_copies[3:]:
            copy.wait()
        work(a, z * n_x + x)
        for s in range(1, n_z):
            def relay(block, way, onward):
                z_copy(a, block, way).wait_recv()

                @pl.when(onward)
                def _():
                    z_copy(a, block, way).start()

                spread(a, block)

            both(s, relay)
            if a == 0 and s == n_z - 1:
                begin(1)
            both(s, lambda block, way, onward: work(a, block * n_x + x))
            both(s - 1, lambda block, way, onward: others(a, block))
        both(n_z - 1, lambda block, way, onward: others(a, block))

    def total(block, carry):
        for a, which in ((0, range(3)), (1, range(3, 4))):
            for i in range(1, n_row):
                r_copy(a, block, me, lax.rem(me + i, n_row)).wait_recv()
            for m in which:
                value = parts[me, block, m].astype(jnp.float32)
                for i in range(1, n_row):
                    value = value + got[lax.rem(me + i, n_row), block, m].astype(jnp.float32)
                sums[m, block] = value.astype(jnp.bfloat16)
        return carry

    lax.fori_loop(0, n_col, total, 0)

    for a in range(2):
        def finish_z(block, carry):
            @pl.when((block <= z) & (z + 1 < n_z))
            def _():
                z_copy(a, block, 0).wait_send()

            @pl.when((block >= z) & (z > 0))
            def _():
                z_copy(a, block, 1).wait_send()

            for i in range(1, n_x):
                x_copy(a, block, x, i).wait_send()
            return carry

        lax.fori_loop(0, n_z, finish_z, 0)

        def finish_block(block, carry):
            out_copy(a, block).wait()
            for i in range(1, n_row):
                r_copy(a, block, lax.rem(me + i, n_row), me).wait_send()
            return carry

        lax.fori_loop(0, n_col, finish_block, 0)


def backward_kernel(
    n_col, n_row, n_z,
    acts, wo, wq, wk, wv,
    block_out, tokens_grad, acts_all,
    held, w_out, w_in, parts, x_got, z_got,
    w_sem, own_sem, g_send, g_recv, x_send, x_recv, z_send, z_recv, out_sem,
):
    n_x, n_y = n_col // n_z, n_row // CORES
    col, me = lax.axis_index("col"), lax.axis_index("row")
    z, x = col // n_x, lax.rem(col, n_x)
    y, core = me // CORES, lax.rem(me, CORES)
    partner = y * CORES + 1 - core
    block_rows = parts.shape[2]
    features = parts.shape[3]
    own_copies = [
        pltpu.make_async_copy(acts.at[m], held.at[m, me], own_sem.at[m]) for m in range(4)
    ]
    for copy in own_copies:
        copy.start()
    weight_copies = [pltpu.make_async_copy(wo, w_out, w_sem.at[0])] + [
        pltpu.make_async_copy(ref, w_in.at[m], w_sem.at[m + 1]) for m, ref in enumerate((wq, wk, wv))
    ]
    for copy in weight_copies:
        copy.start()
    greet(n_col, n_row)

    def g_copy(m, source, slot, to):
        return push(held.at[m, source], held.at[m, source], g_send.at[m, slot],
                    g_recv.at[m, source], "row", to)

    def out_copy(m, source):
        return pltpu.make_async_copy(held.at[m, source], acts_all.at[m, source], out_sem.at[m, source])

    for m in range(4):
        own_copies[m].wait()
        for i in range(1, n_y):
            g_copy(m, me, i, lax.rem(y + i, n_y) * CORES + core).start()
        g_copy(m, me, 0, partner).start()

    def pass_on(m):
        out_copy(m, me).start()
        for i in range(1, n_y):
            source = lax.rem(y + i, n_y) * CORES + core
            g_copy(m, source, 0, partner).wait_recv()
            g_copy(m, source, n_y - 1 + i, partner).start()
            out_copy(m, source).start()

    def settle(m):
        for i in range(n_y):
            source = lax.rem(y + i, n_y) * CORES + 1 - core
            g_copy(m, source, 0, partner).wait_recv()
            out_copy(m, source).start()

    def act(m, block):
        rows = pl.ds(pl.multiple_of(block * block_rows, block_rows), block_rows)
        return jnp.concatenate([held[m, r, rows] for r in range(n_row)], axis=1)

    def x_copy(phase, block, to, source):
        return push(parts.at[phase, block * n_x + to], x_got.at[phase, source, block],
                    x_send.at[phase, block, to], x_recv.at[phase, source, block], "col",
                    z * n_x + to)

    def z_copy(phase, block, way):
        return push(parts.at[phase, block * n_x + x], z_got.at[phase, way, block],
                    z_send.at[phase, block], z_recv.at[phase, way, block], "col",
                    (z + 1 - 2 * way) * n_x + x)

    def multiply(phase, block):
        wide = min(WIDE, features)

        def tile(n, carry):
            cols = pl.ds(pl.multiple_of(n * wide, wide), wide)
            if phase == 0:
                value = jnp.dot(act(0, block), w_out[:, cols], preferred_element_type=jnp.float32)
            else:
                value = contract_cols(act(1, block), w_in[0, cols])
                value = value + contract_cols(act(2, block), w_in[1, cols])
                value = value + contract_cols(act(3, block), w_in[2, cols])
            parts[phase, block, :, cols] = value.astype(jnp.bfloat16)
            return carry

        lax.fori_loop(0, features // wide, tile, 0)

    def farthest_first(distance, fn):
        @pl.when(z + distance < n_z)
        def _():
            fn(z + distance)

        if distance:
            @pl.when(z - distance >= 0)
            def _():
                fn(z - distance)

    def start_phase(phase):
        def send_block(block):
            def send(i, carry):
                to = lax.rem(x + i, n_x)
                multiply(phase, block * n_x + to)
                x_copy(phase, block, to, x).start()
                return carry

            lax.fori_loop(1, n_x, send, 0)
            multiply(phase, block * n_x + x)

        def far(s, carry):
            distance = n_z - 1 - s

            @pl.when(z + distance < n_z)
            def _():
                send_block(z + distance)

            @pl.when(z - distance >= 0)
            def _():
                send_block(z - distance)

            return carry

        lax.fori_loop(0, n_z - 1, far, 0)
        send_block(z)

    def x_total(phase, block):
        value = parts[phase, block * n_x + x].astype(jnp.float32)
        for i in range(1, n_x):
            source = lax.rem(x + i, n_x)
            x_copy(phase, block, x, source).wait_recv()
            value = value + x_got[phase, source, block].astype(jnp.float32)
        parts[phase, block * n_x + x] = value.astype(jnp.bfloat16)

    def add_z(phase, block, way):
        z_copy(phase, block, way).wait_recv()
        slot = block * n_x + x
        parts[phase, slot] = (
            parts[phase, slot].astype(jnp.float32) + z_got[phase, way, block].astype(jnp.float32)
        ).astype(jnp.bfloat16)

    def reduce_step(phase, block):
        x_total(phase, block)

        @pl.when(z < block)
        def _():
            @pl.when(z > 0)
            def _():
                add_z(phase, block, 0)

            z_copy(phase, block, 0).start()

        @pl.when(z > block)
        def _():
            @pl.when(z + 1 < n_z)
            def _():
                add_z(phase, block, 1)

            z_copy(phase, block, 1).start()

    def final(phase, out):
        @pl.when(z > 0)
        def _():
            add_z(phase, z, 0)

        @pl.when(z + 1 < n_z)
        def _():
            add_z(phase, z, 1)

        out[...] = parts[phase, z * n_x + x]

    pass_on(0)
    weight_copies[0].wait()
    settle(0)
    start_phase(0)
    for k in range(n_z):
        if k < 3:
            pass_on(k + 1)
        farthest_first(n_z - 1 - k, functools.partial(reduce_step, 0))
    for m in range(1, 4):
        settle(m)
        weight_copies[m].wait()
    start_phase(1)
    final(0, block_out)
    for k in range(n_z):
        farthest_first(n_z - 1 - k, functools.partial(reduce_step, 1))
    final(1, tokens_grad)

    for m in range(4):
        for i in range(1, n_y):
            g_copy(m, me, i, partner).wait_send()
            g_copy(m, me, n_y - 1 + i, partner).wait_send()
        g_copy(m, me, 0, partner).wait_send()
        for source in range(n_row):
            out_copy(m, source).wait()
    for phase in range(2):
        def finish(block, carry):
            for i in range(1, n_x):
                x_copy(phase, block, lax.rem(x + i, n_x), x).wait_send()

            @pl.when(z != block)
            def _():
                z_copy(phase, block, 0).wait_send()

            return carry

        lax.fori_loop(0, n_z, finish, 0)


def shift_down(value, by):
    return jnp.pad(value, ((by, 0), (0, 0)))[: value.shape[0]] if by else value


def shift_up(value, by):
    return jnp.pad(value, ((0, by), (0, 0)))[by:] if by else value


def local(tokens, query_weight, key_weight, value_weight, out_weight, filter_taps, out_grad):
    n_row, n_col = lax.axis_size("row"), lax.axis_size("col")
    me = lax.axis_index("row")
    n_z, n_x, n_y = Z_LINE, n_col // Z_LINE, n_row // CORES
    block_rows, features = tokens.shape
    hidden = query_weight.shape[1]
    total_tokens = block_rows * n_col
    slice_cols = hidden // n_row
    bf16 = jnp.bfloat16
    anywhere = pl.BlockSpec(memory_space=pl.ANY)
    inside = pl.BlockSpec(memory_space=pltpu.VMEM)
    dma = pltpu.SemaphoreType.DMA
    gathered = jax.ShapeDtypeStruct((n_col, block_rows, features), bf16)
    sums, full_tokens, full_grads = pl.pallas_call(
        functools.partial(forward_kernel, n_col, n_row, n_z),
        out_shape=(
            jax.ShapeDtypeStruct((4, n_col, block_rows, slice_cols), bf16), gathered, gathered,
        ),
        in_specs=[anywhere] * 6,
        out_specs=(inside, anywhere, anywhere),
        scratch_shapes=[
            pltpu.VMEM((2, n_col, block_rows, features), bf16),
            pltpu.VMEM((3, features, hidden), bf16),
            pltpu.VMEM((hidden, features), bf16),
            pltpu.VMEM((n_row, n_col, 4, block_rows, slice_cols), bf16),
            pltpu.VMEM((n_row, n_col, 4, block_rows, slice_cols), bf16),
            dma((2, 2, n_z)), dma((2, n_z)),
            dma((2, n_z, n_x)), dma((2, n_z, n_x)),
            dma((2, n_row, n_col)), dma((2, n_row, n_col)),
            dma((4,)), dma((2,)), dma((2, n_col)),
        ],
        compiler_params=pltpu.CompilerParams(
            collective_id=0, has_side_effects=True, vmem_limit_bytes=VMEM_BYTES
        ),
        name="gather_project",
    )(tokens, out_grad, query_weight, key_weight, value_weight, out_weight)
    full_tokens = full_tokens.reshape(total_tokens, features)
    full_grads = full_grads.reshape(total_tokens, features)
    query, keys, values, gated_grad = [
        sums[m].reshape(total_tokens, slice_cols).astype(jnp.float32) for m in range(4)
    ]
    own_groups = slice_cols // GROUP
    taps = lax.dynamic_slice_in_dim(filter_taps, me * own_groups, own_groups, axis=1)
    taps = jnp.repeat(taps, GROUP, axis=1)
    product = (keys * values).astype(bf16).astype(jnp.float32)
    conv_out = sum(taps[j][None, :] * shift_down(product, j) for j in range(KW))
    conv_out = conv_out.astype(bf16).astype(jnp.float32)
    gated = (query * conv_out).astype(bf16)
    query_back = (gated_grad * conv_out).astype(bf16)
    conv_grad = (gated_grad * query).astype(bf16).astype(jnp.float32)
    product_grad = sum(taps[j][None, :] * shift_up(conv_grad, j) for j in range(KW))
    keys_back = (product_grad * values).astype(bf16)
    values_back = (product_grad * keys).astype(bf16)
    taps_rows = jnp.stack(
        [jnp.sum(conv_grad * shift_down(product, j), axis=0) for j in range(KW)]
    )
    taps_own = taps_rows.reshape(KW, own_groups, GROUP).sum(axis=2)
    taps_grad = lax.all_gather(taps_own, "row", axis=1, tiled=True)
    acts = jnp.stack([gated, query_back, keys_back, values_back])
    shard = jax.ShapeDtypeStruct((block_rows, features), bf16)
    block_out, tokens_grad, acts_all = pl.pallas_call(
        functools.partial(backward_kernel, n_col, n_row, n_z),
        out_shape=(
            shard, shard, jax.ShapeDtypeStruct((4, n_row, total_tokens, slice_cols), bf16),
        ),
        in_specs=[anywhere] * 5,
        out_specs=(inside, inside, anywhere),
        scratch_shapes=[
            pltpu.VMEM((4, n_row, total_tokens, slice_cols), bf16),
            pltpu.VMEM((hidden, features), bf16),
            pltpu.VMEM((3, features, hidden), bf16),
            pltpu.VMEM((2, n_col, block_rows, features), bf16),
            pltpu.VMEM((2, n_x, n_z, block_rows, features), bf16),
            pltpu.VMEM((2, 2, n_z, block_rows, features), bf16),
            dma((4,)), dma((4,)),
            dma((4, 2 * n_y)), dma((4, n_row)),
            dma((2, n_z, n_x)), dma((2, n_x, n_z)),
            dma((2, n_z)), dma((2, 2, n_z)),
            dma((4, n_row)),
        ],
        compiler_params=pltpu.CompilerParams(
            collective_id=1, has_side_effects=True, vmem_limit_bytes=VMEM_BYTES
        ),
        name="gather_scatter",
    )(acts, out_weight, query_weight, key_weight, value_weight)
    joined = jnp.transpose(acts_all, (0, 2, 1, 3)).reshape(4, total_tokens, hidden)
    query_grad = contract_rows(full_tokens, joined[1]).astype(bf16)
    key_grad = contract_rows(full_tokens, joined[2]).astype(bf16)
    value_grad = contract_rows(full_tokens, joined[3]).astype(bf16)
    outw_grad = contract_rows(joined[0], full_grads).astype(bf16)
    return (block_out, tokens_grad, query_grad, key_grad, value_grad, outw_grad, taps_grad)


def solution(mesh):
    in_specs = (
        P("col", "row"),
        P("row", "col"),
        P("row", "col"),
        P("row", "col"),
        P("col", "row"),
        P(None, "col"),
        P("col", "row"),
    )
    out_specs = (
        P("col", "row"),
        P("col", "row"),
        P("row", "col"),
        P("row", "col"),
        P("row", "col"),
        P("col", "row"),
        P(None, "col"),
    )
    return jax.shard_map(local, mesh=mesh, in_specs=in_specs, out_specs=out_specs, check_vma=False)
```

```python
import functools

import jax
import jax.numpy as jnp
from jax import lax
from jax.experimental import pallas as pl
from jax.experimental.pallas import tpu as pltpu
from jax.sharding import PartitionSpec as P

SEQS = 1
KW = 7
GROUP = 16
Z_LINE = 4
CORES = 2
WIDE = 512
MESH = pl.DeviceIdType.MESH
VMEM_BYTES = 62 * 1024 * 1024


def contract_rows(left, right):
    return lax.dot_general(
        left, right, (((0,), (0,)), ((), ())), preferred_element_type=jnp.float32
    )


def contract_cols(left, right):
    return lax.dot_general(
        left, right, (((1,), (1,)), ((), ())), preferred_element_type=jnp.float32
    )


def push(src, dst, send, recv, axis, index):
    return pltpu.make_async_remote_copy(
        src_ref=src,
        dst_ref=dst,
        send_sem=send,
        recv_sem=recv,
        device_id={axis: index},
        device_id_type=MESH,
    )


def greet(n_col, n_row):
    col, row = lax.axis_index("col"), lax.axis_index("row")
    barrier = pltpu.get_barrier_semaphore()
    for i in range(1, n_col):
        pl.semaphore_signal(
            barrier, inc=1, device_id={"col": lax.rem(col + i, n_col)}, device_id_type=MESH
        )
    for i in range(1, n_row):
        pl.semaphore_signal(
            barrier, inc=1, device_id={"row": lax.rem(row + i, n_row)}, device_id_type=MESH
        )
    pl.semaphore_wait(barrier, n_col + n_row - 2)


def forward_kernel(
    n_col, n_row, n_z,
    tokens, grads, wq, wk, wv, wo,
    sums, tokens_all, grads_all,
    held, w_in, w_out, parts, got,
    z_send, z_recv, x_send, x_recv, r_send, r_recv, w_sem, own_sem, out_sem,
):
    n_x = n_col // n_z
    col, me = lax.axis_index("col"), lax.axis_index("row")
    z, x = col // n_x, lax.rem(col, n_x)
    hidden = w_in.shape[2]
    slice_cols = hidden // n_row
    own_copies = [
        pltpu.make_async_copy(ref, held.at[a, col], own_sem.at[a])
        for a, ref in enumerate((tokens, grads))
    ]
    for copy in own_copies:
        copy.start()
    weight_copies = [
        pltpu.make_async_copy(ref, w_in.at[m], w_sem.at[m]) for m, ref in enumerate((wq, wk, wv))
    ] + [pltpu.make_async_copy(wo, w_out, w_sem.at[3])]
    for copy in weight_copies:
        copy.start()
    greet(n_col, n_row)
    own_copies[0].wait()
    own_copies[1].wait()

    def z_copy(a, block, way):
        slot = held.at[a, block * n_x + x]
        return push(slot, slot, z_send.at[a, way, block], z_recv.at[a, block], "col",
                    (z + 1 - 2 * way) * n_x + x)

    def x_copy(a, block, source, i):
        slot = held.at[a, block * n_x + source]
        return push(slot, slot, x_send.at[a, block, i], x_recv.at[a, block, source], "col",
                    z * n_x + lax.rem(x + i, n_x))

    def out_copy(a, block):
        dst = (tokens_all, grads_all)[a]
        return pltpu.make_async_copy(held.at[a, block], dst.at[block], out_sem.at[a, block])

    def r_copy(a, block, to, source):
        which = pl.ds(0, 3) if a == 0 else pl.ds(3, 1)
        return push(parts.at[to, block, which], got.at[source, block, which],
                    r_send.at[a, to, block], r_recv.at[a, source, block], "row", to)

    def work(a, block):
        out_copy(a, block).start()

        def one(m, carry):
            rows = held[a, block]
            if a == 0:
                part = jnp.dot(rows, w_in[m], preferred_element_type=jnp.float32)
            else:
                part = contract_cols(rows, w_out[...])
            part = part.astype(jnp.bfloat16)
            for to in range(n_row):
                parts[to, block, m if a == 0 else 3] = part[:, to * slice_cols:(to + 1) * slice_cols]
            return carry

        if a == 0:
            lax.fori_loop(0, 3, one, 0)
        else:
            one(3, 0)
        for i in range(1, n_row):
            r_copy(a, block, lax.rem(me + i, n_row), me).start()

    def spread(a, block):
        for i in range(1, n_x):
            x_copy(a, block, x, i).start()

    def others(a, block):
        def other(i, carry):
            source = lax.rem(x + i, n_x)
            x_copy(a, block, source, 1).wait_recv()
            work(a, block * n_x + source)
            return carry

        lax.fori_loop(1, n_x, other, 0)

    def begin(a):
        @pl.when(z + 1 < n_z)
        def _():
            z_copy(a, z, 0).start()

        @pl.when(z > 0)
        def _():
            z_copy(a, z, 1).start()

        spread(a, z)

    def both(s, fn):
        @pl.when(z - s >= 0)
        def _():
            fn(z - s, 0, z + 1 < n_z)

        if s != 0:
            @pl.when(z + s < n_z)
            def _():
                fn(z + s, 1, z > 0)

    begin(0)
    for a in range(2):
        for copy in weight_copies[:3] if a == 0 else weight_copies[3:]:
            copy.wait()
        work(a, z * n_x + x)
        for s in range(1, n_z):
            def relay(block, way, onward):
                z_copy(a, block, way).wait_recv()

                @pl.when(onward)
                def _():
                    z_copy(a, block, way).start()

                spread(a, block)

            both(s, relay)
            if a == 0 and s == n_z - 1:
                begin(1)
            both(s, lambda block, way, onward: work(a, block * n_x + x))
            both(s - 1, lambda block, way, onward: others(a, block))
        both(n_z - 1, lambda block, way, onward: others(a, block))

    def total(block, carry):
        for a, which in ((0, range(3)), (1, range(3, 4))):
            for i in range(1, n_row):
                r_copy(a, block, me, lax.rem(me + i, n_row)).wait_recv()
            for m in which:
                value = parts[me, block, m].astype(jnp.float32)
                for i in range(1, n_row):
                    value = value + got[lax.rem(me + i, n_row), block, m].astype(jnp.float32)
                sums[m, block] = value.astype(jnp.bfloat16)
        return carry

    lax.fori_loop(0, n_col, total, 0)

    for a in range(2):
        def finish_z(block, carry):
            @pl.when((block <= z) & (z + 1 < n_z))
            def _():
                z_copy(a, block, 0).wait_send()

            @pl.when((block >= z) & (z > 0))
            def _():
                z_copy(a, block, 1).wait_send()

            for i in range(1, n_x):
                x_copy(a, block, x, i).wait_send()
            return carry

        lax.fori_loop(0, n_z, finish_z, 0)

        def finish_block(block, carry):
            out_copy(a, block).wait()
            for i in range(1, n_row):
                r_copy(a, block, lax.rem(me + i, n_row), me).wait_send()
            return carry

        lax.fori_loop(0, n_col, finish_block, 0)


def backward_kernel(
    n_col, n_row, n_z,
    acts, wo, wq, wk, wv, tokens, grads,
    block_out, tokens_grad, q_grad, k_grad, v_grad, o_grad,
    held, w_out, w_in, parts, x_got, z_got, tokens_in, grads_in, stage, stage_out,
    w_sem, own_sem, g_send, g_recv, x_send, x_recv, z_send, z_recv, out_sem, in_sem,
):
    n_x, n_y = n_col // n_z, n_row // CORES
    col, me = lax.axis_index("col"), lax.axis_index("row")
    z, x = col // n_x, lax.rem(col, n_x)
    y, core = me // CORES, lax.rem(me, CORES)
    partner = y * CORES + 1 - core
    block_rows = parts.shape[2]
    features = parts.shape[3]
    own_copies = [
        pltpu.make_async_copy(acts.at[m], held.at[m, me], own_sem.at[m]) for m in range(4)
    ]
    for copy in own_copies:
        copy.start()
    weight_copies = [pltpu.make_async_copy(wo, w_out, w_sem.at[0])] + [
        pltpu.make_async_copy(ref, w_in.at[m], w_sem.at[m + 1]) for m, ref in enumerate((wq, wk, wv))
    ]
    for copy in weight_copies:
        copy.start()
    late_copies = [
        pltpu.make_async_copy(grads, grads_in, in_sem.at[0]),
        pltpu.make_async_copy(tokens, tokens_in, in_sem.at[1]),
    ]
    for copy in late_copies:
        copy.start()
    greet(n_col, n_row)

    def g_copy(m, source, slot, to):
        return push(held.at[m, source], held.at[m, source], g_send.at[m, slot],
                    g_recv.at[m, source], "row", to)

    for m in range(4):
        own_copies[m].wait()
        for i in range(1, n_y):
            g_copy(m, me, i, lax.rem(y + i, n_y) * CORES + core).start()
        g_copy(m, me, 0, partner).start()

    def pass_on(m):
        for i in range(1, n_y):
            source = lax.rem(y + i, n_y) * CORES + core
            g_copy(m, source, 0, partner).wait_recv()
            g_copy(m, source, n_y - 1 + i, partner).start()

    def settle(m):
        for i in range(n_y):
            source = lax.rem(y + i, n_y) * CORES + 1 - core
            g_copy(m, source, 0, partner).wait_recv()

    def act(m, block):
        rows = pl.ds(pl.multiple_of(block * block_rows, block_rows), block_rows)
        return jnp.concatenate([held[m, r, rows] for r in range(n_row)], axis=1)

    def x_copy(phase, block, to, source):
        return push(parts.at[phase, block * n_x + to],
                    x_got.at[phase, lax.rem(source - to - 1 + n_x, n_x), block],
                    x_send.at[phase, block, to], x_recv.at[phase, source, block], "col",
                    z * n_x + to)

    def z_copy(phase, block, way):
        return push(parts.at[phase, block * n_x + x], z_got.at[phase, way, block],
                    z_send.at[phase, block], z_recv.at[phase, way, block], "col",
                    (z + 1 - 2 * way) * n_x + x)

    def multiply(phase, block):
        wide = min(WIDE, features)

        def tile(n, carry):
            cols = pl.ds(pl.multiple_of(n * wide, wide), wide)
            if phase == 0:
                value = jnp.dot(act(0, block), w_out[:, cols], preferred_element_type=jnp.float32)
            else:
                value = contract_cols(act(1, block), w_in[0, cols])
                value = value + contract_cols(act(2, block), w_in[1, cols])
                value = value + contract_cols(act(3, block), w_in[2, cols])
            parts[phase, block, :, cols] = value.astype(jnp.bfloat16)
            return carry

        lax.fori_loop(0, features // wide, tile, 0)

    def farthest_first(distance, fn):
        @pl.when(z + distance < n_z)
        def _():
            fn(z + distance)

        if distance:
            @pl.when(z - distance >= 0)
            def _():
                fn(z - distance)

    def start_phase(phase):
        def send_block(block):
            def send(i, carry):
                to = lax.rem(x + i, n_x)
                multiply(phase, block * n_x + to)
                x_copy(phase, block, to, x).start()
                return carry

            lax.fori_loop(1, n_x, send, 0)
            multiply(phase, block * n_x + x)

        def far(s, carry):
            distance = n_z - 1 - s

            @pl.when(z + distance < n_z)
            def _():
                send_block(z + distance)

            @pl.when(z - distance >= 0)
            def _():
                send_block(z - distance)

            return carry

        lax.fori_loop(0, n_z - 1, far, 0)
        send_block(z)

    def x_total(phase, block):
        value = parts[phase, block * n_x + x].astype(jnp.float32)
        for i in range(1, n_x):
            source = lax.rem(x + i, n_x)
            x_copy(phase, block, x, source).wait_recv()
            value = value + x_got[phase, i - 1, block].astype(jnp.float32)
        parts[phase, block * n_x + x] = value.astype(jnp.bfloat16)

    def add_z(phase, block, way):
        z_copy(phase, block, way).wait_recv()
        slot = block * n_x + x
        parts[phase, slot] = (
            parts[phase, slot].astype(jnp.float32) + z_got[phase, way, block].astype(jnp.float32)
        ).astype(jnp.bfloat16)

    def reduce_step(phase, block):
        x_total(phase, block)

        @pl.when(z < block)
        def _():
            @pl.when(z > 0)
            def _():
                add_z(phase, block, 0)

            z_copy(phase, block, 0).start()

        @pl.when(z > block)
        def _():
            @pl.when(z + 1 < n_z)
            def _():
                add_z(phase, block, 1)

            z_copy(phase, block, 1).start()

    def final(phase, out):
        @pl.when(z > 0)
        def _():
            add_z(phase, z, 0)

        @pl.when(z + 1 < n_z)
        def _():
            add_z(phase, z, 1)

        out[...] = parts[phase, z * n_x + x]

    rows_out = stage_out.shape[0]
    tile_rows = stage.shape[1]
    per_step = n_row // n_z
    tiles = features // tile_rows // n_z

    def o_copy(r):
        return pltpu.make_async_copy(
            stage_out, o_grad.at[pl.ds(r * rows_out, rows_out)], out_sem.at[3]
        )

    def out_weight_grad(k):
        wide = min(WIDE, features)
        for r in range(k * per_step, (k + 1) * per_step):
            if r:
                o_copy(r - 1).wait()

            def tile(n, carry):
                cols = pl.ds(pl.multiple_of(n * wide, wide), wide)
                stage_out[:, cols] = contract_rows(held[0, r], grads_in[:, cols]).astype(
                    jnp.bfloat16
                )
                return carry

            lax.fori_loop(0, features // wide, tile, 0)
            o_copy(r).start()

    def w_copy(m, n):
        rows = pl.ds(pl.multiple_of(n * tile_rows, tile_rows), tile_rows)
        return pltpu.make_async_copy(
            stage.at[m], (q_grad, k_grad, v_grad)[m].at[rows], out_sem.at[m]
        )

    def in_weight_grads(k):
        def tile(n, carry):
            cols = pl.ds(pl.multiple_of(n * tile_rows, tile_rows), tile_rows)
            left = tokens_in[:, cols]
            for m in range(3):
                @pl.when(n > 0)
                def _():
                    w_copy(m, n - 1).wait()

                stage[m] = jnp.concatenate(
                    [contract_rows(left, held[m + 1, r]).astype(jnp.bfloat16) for r in range(n_row)],
                    axis=1,
                )
                w_copy(m, n).start()
            return carry

        lax.fori_loop(k * tiles, (k + 1) * tiles, tile, 0)

    pass_on(0)
    weight_copies[0].wait()
    settle(0)
    start_phase(0)
    for k in range(n_z):
        if k < 3:
            pass_on(k + 1)
        farthest_first(n_z - 1 - k, functools.partial(reduce_step, 0))
        if k == 0:
            late_copies[0].wait()
        out_weight_grad(k)
    for m in range(1, 4):
        settle(m)
        weight_copies[m].wait()
    start_phase(1)
    final(0, block_out)
    for k in range(n_z):
        if k == 0:
            late_copies[1].wait()
        farthest_first(n_z - 1 - k, functools.partial(reduce_step, 1))
        in_weight_grads(k)
    final(1, tokens_grad)
    o_copy(n_row - 1).wait()
    for m in range(3):
        w_copy(m, features // tile_rows - 1).wait()

    for m in range(4):
        for i in range(1, n_y):
            g_copy(m, me, i, partner).wait_send()
            g_copy(m, me, n_y - 1 + i, partner).wait_send()
        g_copy(m, me, 0, partner).wait_send()
    for phase in range(2):
        def finish(block, carry):
            for i in range(1, n_x):
                x_copy(phase, block, lax.rem(x + i, n_x), x).wait_send()

            @pl.when(z != block)
            def _():
                z_copy(phase, block, 0).wait_send()

            return carry

        lax.fori_loop(0, n_z, finish, 0)


def shift_down(value, by):
    return jnp.pad(value, ((by, 0), (0, 0)))[: value.shape[0]] if by else value


def shift_up(value, by):
    return jnp.pad(value, ((0, by), (0, 0)))[by:] if by else value


def local(tokens, query_weight, key_weight, value_weight, out_weight, filter_taps, out_grad):
    n_row, n_col = lax.axis_size("row"), lax.axis_size("col")
    me = lax.axis_index("row")
    n_z, n_x, n_y = Z_LINE, n_col // Z_LINE, n_row // CORES
    block_rows, features = tokens.shape
    hidden = query_weight.shape[1]
    total_tokens = block_rows * n_col
    slice_cols = hidden // n_row
    bf16 = jnp.bfloat16
    anywhere = pl.BlockSpec(memory_space=pl.ANY)
    inside = pl.BlockSpec(memory_space=pltpu.VMEM)
    dma = pltpu.SemaphoreType.DMA
    gathered = jax.ShapeDtypeStruct((n_col, block_rows, features), bf16)
    sums, full_tokens, full_grads = pl.pallas_call(
        functools.partial(forward_kernel, n_col, n_row, n_z),
        out_shape=(
            jax.ShapeDtypeStruct((4, n_col, block_rows, slice_cols), bf16), gathered, gathered,
        ),
        in_specs=[anywhere] * 6,
        out_specs=(inside, anywhere, anywhere),
        scratch_shapes=[
            pltpu.VMEM((2, n_col, block_rows, features), bf16),
            pltpu.VMEM((3, features, hidden), bf16),
            pltpu.VMEM((hidden, features), bf16),
            pltpu.VMEM((n_row, n_col, 4, block_rows, slice_cols), bf16),
            pltpu.VMEM((n_row, n_col, 4, block_rows, slice_cols), bf16),
            dma((2, 2, n_z)), dma((2, n_z)),
            dma((2, n_z, n_x)), dma((2, n_z, n_x)),
            dma((2, n_row, n_col)), dma((2, n_row, n_col)),
            dma((4,)), dma((2,)), dma((2, n_col)),
        ],
        compiler_params=pltpu.CompilerParams(
            collective_id=0, has_side_effects=True, vmem_limit_bytes=VMEM_BYTES
        ),
        name="gather_project",
    )(tokens, out_grad, query_weight, key_weight, value_weight, out_weight)
    full_tokens = full_tokens.reshape(total_tokens, features)
    full_grads = full_grads.reshape(total_tokens, features)
    query, keys, values, gated_grad = [
        sums[m].reshape(total_tokens, slice_cols).astype(jnp.float32) for m in range(4)
    ]
    own_groups = slice_cols // GROUP
    taps = lax.dynamic_slice_in_dim(filter_taps, me * own_groups, own_groups, axis=1)
    taps = jnp.repeat(taps, GROUP, axis=1)
    product = (keys * values).astype(bf16).astype(jnp.float32)
    conv_out = sum(taps[j][None, :] * shift_down(product, j) for j in range(KW))
    conv_out = conv_out.astype(bf16).astype(jnp.float32)
    gated = (query * conv_out).astype(bf16)
    query_back = (gated_grad * conv_out).astype(bf16)
    conv_grad = (gated_grad * query).astype(bf16).astype(jnp.float32)
    product_grad = sum(taps[j][None, :] * shift_up(conv_grad, j) for j in range(KW))
    keys_back = (product_grad * values).astype(bf16)
    values_back = (product_grad * keys).astype(bf16)
    taps_rows = jnp.stack(
        [jnp.sum(conv_grad * shift_down(product, j), axis=0) for j in range(KW)]
    )
    taps_own = taps_rows.reshape(KW, own_groups, GROUP).sum(axis=2)
    taps_grad = lax.all_gather(taps_own, "row", axis=1, tiled=True)
    acts = jnp.stack([gated, query_back, keys_back, values_back])
    shard = jax.ShapeDtypeStruct((block_rows, features), bf16)
    wide_grad = jax.ShapeDtypeStruct((features, hidden), bf16)
    outs = pl.pallas_call(
        functools.partial(backward_kernel, n_col, n_row, n_z),
        out_shape=(
            shard, shard, wide_grad, wide_grad, wide_grad,
            jax.ShapeDtypeStruct((hidden, features), bf16),
        ),
        in_specs=[anywhere] * 7,
        out_specs=(inside, inside, anywhere, anywhere, anywhere, anywhere),
        scratch_shapes=[
            pltpu.VMEM((4, n_row, total_tokens, slice_cols), bf16),
            pltpu.VMEM((hidden, features), bf16),
            pltpu.VMEM((3, features, hidden), bf16),
            pltpu.VMEM((2, n_col, block_rows, features), bf16),
            pltpu.VMEM((2, n_x - 1, n_z, block_rows, features), bf16),
            pltpu.VMEM((2, 2, n_z, block_rows, features), bf16),
            pltpu.VMEM((total_tokens, features), bf16),
            pltpu.VMEM((total_tokens, features), bf16),
            pltpu.VMEM((3, features // n_z // 2, hidden), bf16),
            pltpu.VMEM((slice_cols, features), bf16),
            dma((4,)), dma((4,)),
            dma((4, 2 * n_y)), dma((4, n_row)),
            dma((2, n_z, n_x)), dma((2, n_x, n_z)),
            dma((2, n_z)), dma((2, 2, n_z)),
            dma((4,)), dma((2,)),
        ],
        compiler_params=pltpu.CompilerParams(
            collective_id=1, has_side_effects=True, vmem_limit_bytes=VMEM_BYTES
        ),
        name="gather_scatter",
    )(acts, out_weight, query_weight, key_weight, value_weight, full_tokens, full_grads)
    return (*outs, taps_grad)


def solution(mesh):
    in_specs = (
        P("col", "row"),
        P("row", "col"),
        P("row", "col"),
        P("row", "col"),
        P("col", "row"),
        P(None, "col"),
        P("col", "row"),
    )
    out_specs = (
        P("col", "row"),
        P("col", "row"),
        P("row", "col"),
        P("row", "col"),
        P("row", "col"),
        P("col", "row"),
        P(None, "col"),
    )
    return jax.shard_map(local, mesh=mesh, in_specs=in_specs, out_specs=out_specs, check_vma=False)
```
